768 devices in a mesh: gx: 96 (over x, y, z_hi), gy: 8 (over z_lo, core).
Axes of the slice: x: 4, y: 8, z: 12 (z_hi: 3, z_lo: 4; z = z_hi * 4 + z_lo), core: 2. Of those that a mesh axis runs over, the one named last changes fastest.
Arguments:
- state: float32 [54, 768, 8192], P(None, 'gx', 'gy'), may hold values from 0.05 to 3, as said below
- diffusivity: float32 [54], replicated, may hold values from 0.02 to 0.1
- log_prefactor: float32 [325], replicated, may hold values from -1 to 1
- activation: float32 [325], replicated, may hold values from 0.5 to 4
- heat: float32 [325], replicated, may hold values from 0.005 to 0.05
- reactants: float32 [650, 53], replicated, may hold values from 0 to 1, as said below
- products: float32 [53, 325], replicated, may hold values from 0 to 2, as said below
- substeps: int32 [768, 64], P('gx', 'gy'), may hold values from 1 to 4
- flame: int32 [768, 64], P('gx', 'gy'), may hold values from 0 to 1, as said below
Outputs:
- next_state: float32 [54, 768, 8192], P(None, 'gx', 'gy')
The draws below stay inside these ranges and needn't reach their ends.
Inputs may be any that keep to these rules, and one draw needn't show every extreme that they name: `state`: component 0 is the temperature, from 1 to 3; the other components are concentrations from 0.05 to 2. `reactants`: each row is one-hot: it names one species. `products`: column r is the sum of two one-hot columns, the two products of reaction r. `flame`: within the 8 x (8) entries that one device holds, at most 8 are 1. In every draw there is one index along the first mesh axis where every device holds exactly 8; elsewhere a device holds 8 with probability 1/4 and otherwise 0 to 2.
All inputs are finite; a program needn't handle non-finite values.
Results may differ from the reference program's by a relative error of at most 0.0001.
Values sent between devices are 32-bit elements; how exact they have to be, the bound alone decides.
A program may use at most 128 MiB of HBM per device.

```python
import math
import jax
import jax.numpy as jnp
from jax import lax

SP = 53
RX = 325
COMP = 54
X_DEV = 8
Y_DEV = 32
NZ = 32
BLOCK = 128
MAXSUB = 4
NX = 768
NY = 256
NBY = 64


def draw_state(key, part):
    shape = (SP + 1, NX, NY * NZ)
    uniform = jax.random.uniform(key, shape, jnp.float32)
    first_row = jnp.arange(SP + 1) == 0
    lower = jnp.where(first_row, 1.0, 0.05)[:, None, None]
    upper = jnp.where(first_row, 3.0, 2.0)[:, None, None]
    return jnp.exp(jnp.log(lower) + (jnp.log(upper) - jnp.log(lower)) * uniform)


def draw_reactants(key, part):
    chosen = jax.random.randint(jax.random.fold_in(key, 11), (2 * RX,), 0, SP)
    return (chosen[:, None] == jnp.arange(SP)[None, :]).astype(jnp.float32)


def draw_products(key, part):
    chosen = jax.random.randint(jax.random.fold_in(key, 23), (2, RX), 0, SP)
    species = jnp.arange(SP)[:, None]
    return (species == chosen[0][None, :]).astype(jnp.float32) + (species == chosen[1][None, :]).astype(jnp.float32)


def draw_flame(key, part):
    columns = NX // X_DEV
    rows = NY // Y_DEV
    row_blocks = Y_DEV * NZ // BLOCK
    per_device = X_DEV * row_blocks
    most = rows
    keys = jax.random.split(jax.random.fold_in(key, 37), 4)
    heavy = jax.random.randint(keys[0], (columns, rows), 0, 4) == 0
    light = jnp.minimum(jax.random.randint(keys[1], (columns, rows), 0, 3), most)
    counted = jnp.where(heavy, most, light)
    full_column = jax.random.randint(keys[2], (), 0, columns)
    counted = jnp.where(jnp.arange(columns)[:, None] == full_column, most, counted)
    block_ratings = jax.random.randint(keys[3], (columns, rows, per_device), 0, 65536) * per_device + jnp.arange(per_device)
    ranks = jnp.argsort(jnp.argsort(block_ratings, axis=-1), axis=-1)
    burning = (ranks < counted[..., None]).astype(jnp.int32)
    burning = burning.reshape(columns, rows, X_DEV, row_blocks)
    return jnp.transpose(burning, (0, 2, 1, 3)).reshape(NX, rows * row_blocks)


def place_ends(entries, stream_key, low, high):
    index_at = [jax.random.randint(jax.random.fold_in(stream_key, axis), (), 0, length) for axis, length in enumerate(entries.shape)]
    widest = entries.shape.index(max(entries.shape))
    next_to = index_at[:widest] + [(index_at[widest] + 1) % entries.shape[widest]] + index_at[widest + 1:]
    return entries.at[tuple(index_at)].set(low).at[tuple(next_to)].set(high)


def setup_inputs(seed: int = 0) -> dict:
    key_of = jax.random.split(jax.random.key(seed), 10)
    return {
        "state": draw_state(jax.random.fold_in(key_of[9], 71), 0),
        "diffusivity": jnp.clip(jnp.exp(jax.random.uniform(key_of[1], (COMP,), jnp.float32, math.log(0.02), math.log(0.1))), 0.02, 0.1),
        "log_prefactor": jnp.clip(jax.random.uniform(key_of[2], (RX,), jnp.float32, -1.0, 1.0), -1.0, 1.0),
        "activation": jnp.clip(jnp.exp(jax.random.uniform(key_of[3], (RX,), jnp.float32, math.log(0.5), math.log(4.0))), 0.5, 4.0),
        "heat": jnp.clip(jnp.exp(jax.random.uniform(key_of[4], (RX,), jnp.float32, math.log(0.005), math.log(0.05))), 0.005, 0.05),
        "reactants": draw_reactants(jax.random.fold_in(key_of[9], 71), 0),
        "products": draw_products(jax.random.fold_in(key_of[9], 71), 0),
        "substeps": place_ends(jax.random.randint(key_of[7], (NX, NBY), 1, MAXSUB + 1), jax.random.fold_in(key_of[7], 1), 1, MAXSUB).astype(jnp.int32),
        "flame": draw_flame(jax.random.fold_in(key_of[9], 71), 0),
    }


near_weight = 4.0 / 3.0
far_weight = 1.0 / 12.0
centre_weight = 7.5


def along_z(field, offset, zposition):
    if offset > 0:
        return jnp.where(zposition < NZ - offset, jnp.roll(field, -offset, -1), jnp.roll(field, NZ - offset, -1))
    reach = -offset
    return jnp.where(zposition >= reach, jnp.roll(field, reach, -1), jnp.roll(field, reach - NZ, -1))


def laplacian(field, zposition):
    nearest = jnp.roll(field, 1, 0) + jnp.roll(field, -1, 0)
    nearest = nearest + jnp.roll(field, NZ, 1) + jnp.roll(field, -NZ, 1)
    nearest = nearest + along_z(field, 1, zposition) + along_z(field, -1, zposition)
    farther = jnp.roll(field, 2, 0) + jnp.roll(field, -2, 0)
    farther = farther + jnp.roll(field, 2 * NZ, 1) + jnp.roll(field, -2 * NZ, 1)
    farther = farther + along_z(field, 2, zposition) + along_z(field, -2, zposition)
    return near_weight * nearest - far_weight * farther - centre_weight * field


def react_step(thermal, amounts, step_size, log_prefactor, activation, heat, reactants, products):
    exact_result = lax.Precision.HIGHEST
    nreact = log_prefactor.shape[0]
    speeds = jnp.exp(log_prefactor[:, None] - activation[:, None] / thermal[..., None, :])
    picked = jnp.einsum('qs,...sn->...qn', reactants, amounts, precision=exact_result)
    first_side = picked[..., :nreact, :]
    second_side = picked[..., nreact:, :]
    progress = speeds * first_side * second_side
    produced = jnp.einsum('sr,...rn->...sn', products, progress, precision=exact_result)
    partner = jnp.concatenate([speeds * second_side, speeds * first_side], axis=-2)
    consumed = jnp.einsum('qs,...qn->...sn', reactants, partner, precision=exact_result)
    widened = step_size[..., None, :]
    new_amounts = (amounts + widened * produced) / (1.0 + widened * consumed)
    new_thermal = thermal + step_size * jnp.einsum('r,...rn->...n', heat, progress, precision=exact_result)
    return new_thermal, new_amounts


def reference(state, diffusivity, log_prefactor, activation, heat, reactants, products, substeps, flame):
    components, planes, row_cells = state.shape
    zposition = jnp.arange(row_cells) % NZ
    transport = lax.map(lambda field: laplacian(field, zposition), state) * diffusivity[:, None, None]
    live = (flame * substeps).reshape(-1).astype(jnp.int32)
    block_list = state.reshape(components, -1, BLOCK)

    def per_block(inputs):
        position, count = inputs
        block = lax.dynamic_index_in_dim(block_list, position, 1, keepdims=False)
        step_size = jnp.reshape(1.0 / jnp.maximum(count, 1).astype(jnp.float32), (1,))

        def advance(substep, carry):
            return react_step(carry[0], carry[1], step_size, log_prefactor, activation, heat, reactants, products)

        thermal, amounts = lax.fori_loop(0, count, advance, (block[0], block[1:]))
        return jnp.concatenate([thermal[None], amounts], 0)

    reacted = lax.map(per_block, (jnp.arange(live.shape[0], dtype=jnp.int32), live))
    reacted = jnp.transpose(reacted, (1, 0, 2)).reshape(components, planes, row_cells)
    return reacted + transport
```

```python
import functools

import jax
import jax.numpy as jnp
from jax import lax
from jax.experimental import pallas as pl
from jax.experimental.pallas import tpu as pltpu
from jax.sharding import PartitionSpec as P

NZ = 32
BLOCK = 128
MAXSUB = 4
SLOTS = 8
SP = 53
COMP = 54
RX = 325
CROWS = 64
RROWS = 336
RPAD = 384
WIDE = 256
HALF = COMP // 2
CHUNKS = ((0, 9), (9, 9), (18, 9), (27, 9), (36, 9), (45, 9))

near_weight = 4.0 / 3.0
far_weight = 1.0 / 12.0
centre_weight = 7.5

MESH = pl.DeviceIdType.MESH
F32 = jnp.float32
BF16 = jnp.bfloat16


def split2(x):
    high = x.astype(BF16)
    return high, (x - high.astype(F32)).astype(BF16)


def split3(x):
    high = x.astype(BF16)
    rest = x - high.astype(F32)
    middle = rest.astype(BF16)
    return high, middle, (rest - middle.astype(F32)).astype(BF16)


def kernel(
    n, m,
    state, diffusivity, log_prefactor, activation, heat, reactants_t, products, substeps, flame,
    out,
    S, H, YS, YR, DF, LP, AC, HT, RT, PT, SB, FL,
    LB, AB, RA, RB, C, PP, A, Q, CN, ST, Z, LV, RK,
    x_send, x_recv, y_send, y_recv, local,
):
    gx, gy = lax.axis_index("gx"), lax.axis_index("gy")
    right, left = lax.rem(gx + 1, n), lax.rem(gx + n - 1, n)
    up, down = lax.rem(gy + 1, m), lax.rem(gy + m - 1, m)

    barrier = pltpu.get_barrier_semaphore()
    for device in ((right, gy), (left, gy), (gx, up), (gx, down)):
        pl.semaphore_signal(barrier, inc=1, device_id=device, device_id_type=MESH)

    loads = [
        pltpu.make_async_copy(state, S, local.at[0]),
        pltpu.make_async_copy(diffusivity, DF, local.at[1]),
        pltpu.make_async_copy(log_prefactor, LP, local.at[2]),
        pltpu.make_async_copy(activation, AC, local.at[3]),
        pltpu.make_async_copy(heat, HT, local.at[4]),
        pltpu.make_async_copy(reactants_t, RT, local.at[5]),
        pltpu.make_async_copy(products, PT, local.at[6]),
        pltpu.make_async_copy(substeps, SB, local.at[7]),
        pltpu.make_async_copy(flame, FL, local.at[8]),
    ]
    for load in loads:
        load.start()

    pl.semaphore_wait(barrier, 4)
    x_copies = []
    for k, (c0, cn) in enumerate(CHUNKS):
        pair = (
            pltpu.make_async_remote_copy(
                state.at[c0 : c0 + cn, 6:8, :], H.at[c0 : c0 + cn, 6:8, :],
                x_send.at[0, k], x_recv.at[0, k], device_id=(right, gy), device_id_type=MESH,
            ),
            pltpu.make_async_remote_copy(
                state.at[c0 : c0 + cn, 0:2, :], H.at[c0 : c0 + cn, 0:2, :],
                x_send.at[1, k], x_recv.at[1, k], device_id=(left, gy), device_id_type=MESH,
            ),
        )
        for copy in pair:
            copy.start()
        x_copies.append(pair)
    loads[0].wait()
    lane = lax.broadcasted_iota(jnp.int32, (8, BLOCK), 1)
    sub = lax.broadcasted_iota(jnp.int32, (8, BLOCK), 0)

    def pack(c, _):
        YS[0, c] = jnp.where(
            lane < 64,
            pltpu.roll(S[c, :, 896:1024], 64, 1),
            S[c + HALF, :, 896:1024],
        )
        YS[1, c] = jnp.where(
            lane < 64,
            S[c, :, 0:128],
            pltpu.roll(S[c + HALF, :, 0:128], 64, 1),
        )
        return 0

    lax.fori_loop(0, HALF, pack, 0)

    y_copies = [
        pltpu.make_async_remote_copy(
            YS.at[0], YR.at[0], y_send.at[0], y_recv.at[0], device_id=(gx, up), device_id_type=MESH
        ),
        pltpu.make_async_remote_copy(
            YS.at[1], YR.at[1], y_send.at[1], y_recv.at[1], device_id=(gx, down), device_id_type=MESH
        ),
    ]
    for copy in y_copies:
        copy.start()

    for load in loads[1:]:
        load.wait()

    def column(row):
        padded = jnp.concatenate([row, jnp.zeros((1, RPAD - RX), F32)], axis=1)
        turned = jnp.broadcast_to(padded, (BLOCK, RPAD)).T
        return turned[0:RROWS]

    for source, target in ((LP, LB), (AC, AB)):
        value = column(source[...].reshape(1, RX))
        target[:, 0:BLOCK] = value
        target[:, BLOCK:WIDE] = value

    def placed(value):
        wide = jnp.concatenate([value, jnp.zeros((SP, RPAD - RX), F32)], axis=1)
        return jnp.concatenate(
            [jnp.zeros((1, RPAD), F32), wide, jnp.zeros((CROWS - COMP, RPAD), F32)], axis=0
        )

    table = RT[...]
    first = placed(table[:, 0:RX])
    second = placed(table[:, RX : 2 * RX])
    for value, target in ((first, RA), (second, RB)):
        stacked = jnp.concatenate([value, value, value, jnp.zeros_like(value)], axis=0)
        target[...] = stacked.T[0:RROWS].astype(BF16)
    for k, value in enumerate((first, first, second, second)):
        C[:, k * RPAD : (k + 1) * RPAD] = value.astype(BF16)
    heat_row = jnp.concatenate([HT[...].reshape(1, RX), jnp.zeros((1, RPAD - RX), F32)], axis=1)
    heat_high, heat_mid, heat_low = split3(heat_row)
    row = lax.broadcasted_iota(jnp.int32, (CROWS, RPAD), 0)
    stoich = placed(PT[...])
    for at, piece in ((0, heat_high), (COMP, heat_mid), (COMP + 1, heat_low)):
        stoich = jnp.where(row == at, piece.astype(F32), stoich)
    PP[:, 0:RPAD] = stoich.astype(BF16)
    PP[:, RPAD : 2 * RPAD] = stoich.astype(BF16)
    Z[...] = jnp.zeros_like(Z)
    A[...] = jnp.zeros_like(A)

    before = jnp.zeros((8, BLOCK), jnp.int32)
    slot_plane = jnp.zeros((8, BLOCK), jnp.int32)
    slot_tile = jnp.zeros((8, BLOCK), jnp.int32) - 1
    slot_count = jnp.zeros((8, BLOCK), jnp.int32)
    burning = FL[...]
    counts = SB[...]
    for t in range(8):
        for x in range(8):
            lit = jnp.broadcast_to(burning[x : x + 1, t : t + 1], (8, BLOCK))
            steps = jnp.broadcast_to(counts[x : x + 1, t : t + 1], (8, BLOCK))
            match = (lit == 1) & (before == sub)
            slot_plane = jnp.where(match, x, slot_plane)
            slot_tile = jnp.where(match, t, slot_tile)
            slot_count = jnp.where(match, steps, slot_count)
            LV[t, x : x + 1, :] = lit[0:1]
            RK[t, x : x + 1, :] = jnp.minimum(before, SLOTS - 1)[0:1]
            before = before + lit
    step_size = 1.0 / jnp.maximum(slot_count, 1).astype(F32)
    for v in range(SLOTS):
        CN[:, v * BLOCK : (v + 1) * BLOCK] = jnp.broadcast_to(slot_count[v : v + 1], (8, BLOCK))
        ST[:, v * BLOCK : (v + 1) * BLOCK] = jnp.broadcast_to(step_size[v : v + 1], (8, BLOCK))

    def gather(c, _):
        value = jnp.zeros((8, BLOCK), F32) + 1.0
        for t in range(8):
            tile = S[c, :, t * BLOCK : (t + 1) * BLOCK]
            value = jnp.where(slot_tile == t, jnp.take_along_axis(tile, slot_plane, axis=0), value)
        Q[c] = value
        return 0

    lax.fori_loop(0, COMP, gather, 0)
    for v in range(SLOTS):
        A[0:COMP, v * BLOCK : (v + 1) * BLOCK] = Q[:, v, :]

    component = lax.broadcasted_iota(jnp.int32, (CROWS, WIDE), 0)

    def group(g, _):
        at = pl.ds(pl.multiple_of(g * WIDE, WIDE), WIDE)

        def substep(t, _):
            amounts = A[:, at]
            inverse = 1.0 / amounts[0:1]
            speeds = jnp.exp(LB[...] - AB[...] * inverse)
            pieces = split3(amounts)
            operand = jnp.concatenate([*pieces, jnp.zeros_like(pieces[0])], axis=0)
            first_side = jnp.dot(RA[...], operand, preferred_element_type=F32)
            second_side = jnp.dot(RB[...], operand, preferred_element_type=F32)
            to_first = speeds * second_side
            to_second = speeds * first_side
            progress = to_second * second_side
            for k, value in enumerate((to_first, to_second, progress)):
                high, low = split2(value)
                Z[2 * k * RPAD : 2 * k * RPAD + RROWS, :] = high
                Z[(2 * k + 1) * RPAD : (2 * k + 1) * RPAD + RROWS, :] = low
            consumed = jnp.dot(C[...], Z[0 : 4 * RPAD, :], preferred_element_type=F32)
            produced = jnp.dot(PP[...], Z[4 * RPAD : 6 * RPAD, :], preferred_element_type=F32)
            warmed = produced[0:1] + produced[COMP : COMP + 1] + produced[COMP + 1 : COMP + 2]
            produced = jnp.where(component == 0, warmed, produced)
            step = ST[0:1, at]
            updated = (amounts + step * produced) / (1.0 + step * consumed)
            active = (t < CN[0:1, at]) & (component < COMP)
            A[:, at] = jnp.where(active, updated, amounts)
            return 0

        lax.fori_loop(0, MAXSUB, substep, 0)
        return 0

    lax.fori_loop(0, SLOTS * BLOCK // WIDE, group, 0)
    for v in range(SLOTS):
        Q[:, v, :] = A[0:COMP, v * BLOCK : (v + 1) * BLOCK]

    zpos = lane % NZ

    def along_z(tile, offset):
        if offset > 0:
            return jnp.where(
                zpos < NZ - offset, pltpu.roll(tile, BLOCK - offset, 1), pltpu.roll(tile, NZ - offset, 1)
            )
        reach = -offset
        return jnp.where(zpos >= reach, pltpu.roll(tile, reach, 1), pltpu.roll(tile, BLOCK + reach - NZ, 1))

    def inner(c, _):
        weight = DF[0, c]
        done = Q[c]
        tiles = [S[c, :, t * BLOCK : (t + 1) * BLOCK] for t in range(8)]
        plus = [pltpu.roll(x, BLOCK - NZ, 1) for x in tiles]
        minus = [pltpu.roll(x, NZ, 1) for x in tiles]
        half = [pltpu.roll(x, 2 * NZ, 1) for x in tiles]
        zero = jnp.zeros((8, BLOCK), F32)
        for t, x in enumerate(tiles):
            before_y = minus[t - 1] if t > 0 else zero
            after_y = plus[t + 1] if t < 7 else zero
            before_y2 = half[t - 1] if t > 0 else zero
            after_y2 = half[t + 1] if t < 7 else zero
            near = jnp.where(lane >= NZ, minus[t], before_y) + jnp.where(lane < BLOCK - NZ, plus[t], after_y)
            far = jnp.where(lane >= 2 * NZ, half[t], before_y2) + jnp.where(lane < 2 * NZ, half[t], after_y2)
            near = near + (along_z(x, 1) + along_z(x, -1))
            far = far + (along_z(x, 2) + along_z(x, -2))
            near = near + (
                jnp.where(sub >= 1, pltpu.roll(x, 1, 0), 0.0) + jnp.where(sub < 7, pltpu.roll(x, 7, 0), 0.0)
            )
            far = far + (
                jnp.where(sub >= 2, pltpu.roll(x, 2, 0), 0.0) + jnp.where(sub < 6, pltpu.roll(x, 6, 0), 0.0)
            )
            reacted = jnp.where(LV[t] == 1, jnp.take_along_axis(done, RK[t], axis=0), x)
            out[c, :, t * BLOCK : (t + 1) * BLOCK] = reacted + weight * (
                near_weight * near - far_weight * far - centre_weight * x
            )
        return 0

    lax.fori_loop(0, COMP, inner, 0)

    for copy in y_copies:
        copy.wait_recv()

    def edges(c, _):
        low, high = YR[0, c], YR[1, c]
        for comp, lo, hi in (
            (c, low, pltpu.roll(high, 64, 1)),
            (c + HALF, pltpu.roll(low, 64, 1), high),
        ):
            weight = DF[0, comp]
            near = jnp.where(lane < NZ, pltpu.roll(lo, BLOCK - NZ, 1), 0.0)
            far = jnp.where(lane < 2 * NZ, lo, 0.0)
            out[comp, :, 0:128] += weight * (near_weight * near - far_weight * far)
            near = jnp.where(lane >= BLOCK - NZ, pltpu.roll(hi, NZ, 1), 0.0)
            far = jnp.where(lane >= 2 * NZ, hi, 0.0)
            out[comp, :, 896:1024] += weight * (near_weight * near - far_weight * far)
        return 0

    lax.fori_loop(0, HALF, edges, 0)

    sub_row = lax.broadcasted_iota(jnp.int32, (8, 1024), 0)

    def outer(c, _):
        weight = DF[0, c]
        x = H[c]
        near = jnp.where(
            sub_row == 0, pltpu.roll(x, 1, 0), jnp.where(sub_row == 7, pltpu.roll(x, 7, 0), 0.0)
        )
        far = jnp.where(
            sub_row < 2, pltpu.roll(x, 2, 0), jnp.where(sub_row >= 6, pltpu.roll(x, 6, 0), 0.0)
        )
        out[c] += weight * (near_weight * near - far_weight * far)
        return 0

    for (c0, cn), pair in zip(CHUNKS, x_copies):
        for copy in pair:
            copy.wait_recv()
        lax.fori_loop(c0, c0 + cn, outer, 0)

    for pair in x_copies:
        for copy in pair:
            copy.wait_send()
    for copy in y_copies:
        copy.wait_send()


def per_device(
    state, diffusivity, log_prefactor, activation, heat, reactants, products, substeps, flame
):
    n, m = lax.axis_size("gx"), lax.axis_size("gy")
    anywhere = pl.BlockSpec(memory_space=pl.ANY)
    vmem, smem, dma = pltpu.VMEM, pltpu.SMEM, pltpu.SemaphoreType.DMA
    cells = state.shape[2]
    return pl.pallas_call(
        functools.partial(kernel, n, m),
        out_shape=pltpu.VMEM(state.shape, F32),
        in_specs=[anywhere] * 9,
        out_specs=pl.BlockSpec(memory_space=pltpu.VMEM),
        scratch_shapes=[
            vmem((COMP, 8, cells), F32),
            vmem((COMP, 8, cells), F32),
            vmem((2, HALF, 8, BLOCK), F32),
            vmem((2, HALF, 8, BLOCK), F32),
            smem((1, COMP), F32),
            vmem((RX,), F32),
            vmem((RX,), F32),
            vmem((RX,), F32),
            vmem((SP, 2 * RX), F32),
            vmem((SP, RX), F32),
            vmem((8, 8), jnp.int32),
            vmem((8, 8), jnp.int32),
            vmem((RROWS, WIDE), F32),
            vmem((RROWS, WIDE), F32),
            vmem((RROWS, 4 * CROWS), BF16),
            vmem((RROWS, 4 * CROWS), BF16),
            vmem((CROWS, 4 * RPAD), BF16),
            vmem((CROWS, 2 * RPAD), BF16),
            vmem((CROWS, SLOTS * BLOCK), F32),
            vmem((COMP, SLOTS, BLOCK), F32),
            vmem((8, SLOTS * BLOCK), jnp.int32),
            vmem((8, SLOTS * BLOCK), F32),
            vmem((6 * RPAD, WIDE), BF16),
            vmem((8, 8, BLOCK), jnp.int32),
            vmem((8, 8, BLOCK), jnp.int32),
            dma((2, len(CHUNKS))), dma((2, len(CHUNKS))), dma((2,)), dma((2,)), dma((9,)),
        ],
        compiler_params=pltpu.CompilerParams(
            collective_id=0, has_side_effects=True, vmem_limit_bytes=VMEM_LIMIT
        ),
    )(
        state, diffusivity.reshape(1, -1), log_prefactor, activation,
        heat, reactants.T, products, substeps, flame,
    )


VMEM_LIMIT = 60 << 20


def solution(mesh):
    in_specs = (P(None, "gx", "gy"), P(), P(), P(), P(), P(), P(), P("gx", "gy"), P("gx", "gy"))
    return jax.shard_map(
        per_device, mesh=mesh, in_specs=in_specs, out_specs=P(None, "gx", "gy"), check_vma=False
    )
```

```python
import functools

import jax
import jax.numpy as jnp
from jax import lax
from jax.experimental import pallas as pl
from jax.experimental.pallas import tpu as pltpu
from jax.sharding import PartitionSpec as P

NZ = 32
BLOCK = 128
MAXSUB = 4
SLOTS = 8
SP = 53
COMP = 54
RX = 325
CROWS = 64
RROWS = 336
RPAD = 384
WIDE = 256
HALF = COMP // 2
CHUNKS = ((0, 9), (9, 9), (18, 9), (27, 9), (36, 9), (45, 9))

near_weight = 4.0 / 3.0
far_weight = 1.0 / 12.0
centre_weight = 7.5

MESH = pl.DeviceIdType.MESH
F32 = jnp.float32
BF16 = jnp.bfloat16


def split2(x):
    high = x.astype(BF16)
    return high, (x - high.astype(F32)).astype(BF16)


def split3(x):
    high = x.astype(BF16)
    rest = x - high.astype(F32)
    middle = rest.astype(BF16)
    return high, middle, (rest - middle.astype(F32)).astype(BF16)


def looped(first, count, body, together):
    def step(i, _):
        for k in range(together):
            body(first + i * together + k, 0)
        return 0

    lax.fori_loop(0, count // together, step, 0)


def kernel(
    n, m,
    state, diffusivity, log_prefactor, activation, heat, reactants_t, products, substeps, flame,
    out,
    S, H, YS, YR, DF, LP, AC, HT, RT, PT, SB, FL,
    LB, AB, RA, RB, C, PP, A, Q, CN, ST, Z, LV, RK,
    x_send, x_recv, y_send, y_recv, local,
):
    gx, gy = lax.axis_index("gx"), lax.axis_index("gy")
    right, left = lax.rem(gx + 1, n), lax.rem(gx + n - 1, n)
    up, down = lax.rem(gy + 1, m), lax.rem(gy + m - 1, m)

    barrier = pltpu.get_barrier_semaphore()
    part = lax.rem(gx, 3)

    def greet(device):
        pl.semaphore_signal(barrier, inc=1, device_id=device, device_id_type=MESH)

    greet((gx, up))
    greet((gx, down))

    @pl.when(part == 0)
    def _():
        greet((right, gy))

    @pl.when(part == 1)
    def _():
        greet((left, gy))


    loads = [
        pltpu.make_async_copy(state, S, local.at[0]),
        pltpu.make_async_copy(diffusivity, DF, local.at[1]),
        pltpu.make_async_copy(log_prefactor, LP, local.at[2]),
        pltpu.make_async_copy(activation, AC, local.at[3]),
        pltpu.make_async_copy(heat, HT, local.at[4]),
        pltpu.make_async_copy(reactants_t, RT, local.at[5]),
        pltpu.make_async_copy(products, PT, local.at[6]),
        pltpu.make_async_copy(substeps, SB, local.at[7]),
        pltpu.make_async_copy(flame, FL, local.at[8]),
    ]
    for load in loads:
        load.start()

    @pl.when(part == 0)
    def _():
        pl.semaphore_wait(barrier, 3)
        greet((left, gy))

    @pl.when(part == 1)
    def _():
        pl.semaphore_wait(barrier, 3)
        greet((right, gy))

    @pl.when(part == 2)
    def _():
        pl.semaphore_wait(barrier, 4)
        greet((right, gy))
        greet((left, gy))

    x_copies = []
    for k, (c0, cn) in enumerate(CHUNKS):
        pair = (
            pltpu.make_async_remote_copy(
                state.at[c0 : c0 + cn, 6:8, :], H.at[c0 : c0 + cn, 6:8, :],
                x_send.at[0, k], x_recv.at[0, k], device_id=(right, gy), device_id_type=MESH,
            ),
            pltpu.make_async_remote_copy(
                state.at[c0 : c0 + cn, 0:2, :], H.at[c0 : c0 + cn, 0:2, :],
                x_send.at[1, k], x_recv.at[1, k], device_id=(left, gy), device_id_type=MESH,
            ),
        )
        x_copies.append(pair)

    place = gy // 2

    @pl.when((part == 1) & (place < 3))
    def _():
        x_copies[0][1].start()
        x_copies[1][1].start()

    @pl.when((part == 2) & (place < 3))
    def _():
        x_copies[0][0].start()
        x_copies[1][0].start()
        x_copies[0][1].start()

    @pl.when((part == 2) & (place == 3))
    def _():
        x_copies[0][1].start()

    loads[0].wait()
    lane = lax.broadcasted_iota(jnp.int32, (8, BLOCK), 1)
    sub = lax.broadcasted_iota(jnp.int32, (8, BLOCK), 0)

    def pack(c, _):
        YS[0, c] = jnp.where(
            lane < 64,
            pltpu.roll(S[c, :, 896:1024], 64, 1),
            S[c + HALF, :, 896:1024],
        )
        YS[1, c] = jnp.where(
            lane < 64,
            S[c, :, 0:128],
            pltpu.roll(S[c + HALF, :, 0:128], 64, 1),
        )
        return 0

    looped(0, HALF, pack, 3)

    y_copies = [
        pltpu.make_async_remote_copy(
            YS.at[0], YR.at[0], y_send.at[0], y_recv.at[0], device_id=(gx, up), device_id_type=MESH
        ),
        pltpu.make_async_remote_copy(
            YS.at[1], YR.at[1], y_send.at[1], y_recv.at[1], device_id=(gx, down), device_id_type=MESH
        ),
    ]
    @pl.when(part == 0)
    def _():
        y_copies[0].start()
        y_copies[1].start()
        x_copies[0][0].start()
        x_copies[1][0].start()
        x_copies[2][0].start()
        x_copies[3][0].start()
        x_copies[4][0].start()
        x_copies[5][0].start()

    @pl.when((part == 1) & (place < 3))
    def _():
        y_copies[0].start()
        y_copies[1].start()
        x_copies[2][1].start()
        x_copies[3][1].start()
        x_copies[4][1].start()
        x_copies[5][1].start()

    @pl.when((part == 1) & (place == 3))
    def _():
        y_copies[0].start()
        y_copies[1].start()

    @pl.when((part == 2) & (place < 3))
    def _():
        y_copies[0].start()
        y_copies[1].start()
        x_copies[2][0].start()
        x_copies[1][1].start()
        x_copies[3][0].start()
        x_copies[2][1].start()
        x_copies[4][0].start()
        x_copies[3][1].start()
        x_copies[5][0].start()
        x_copies[4][1].start()
        x_copies[5][1].start()

    @pl.when((part == 2) & (place == 3))
    def _():
        y_copies[0].start()
        y_copies[1].start()
        x_copies[1][1].start()
        x_copies[2][1].start()
        x_copies[3][1].start()
        x_copies[4][1].start()
        x_copies[5][1].start()

    @pl.when(part < 2)
    def _():
        pl.semaphore_wait(barrier, 1)

    @pl.when(part == 0)
    def _():
        x_copies[0][1].start()
        x_copies[1][1].start()
        x_copies[2][1].start()
        x_copies[3][1].start()
        x_copies[4][1].start()
        x_copies[5][1].start()

    @pl.when((part == 1) & (place < 3))
    def _():
        x_copies[0][0].start()
        x_copies[1][0].start()
        x_copies[2][0].start()
        x_copies[3][0].start()
        x_copies[4][0].start()
        x_copies[5][0].start()

    def checkpoint(at):

        @pl.when(((part == 2) & (place == 3)) & (at == 17))
        def _():
            x_copies[0][0].start()
            x_copies[1][0].start()
            x_copies[2][0].start()
            x_copies[3][0].start()
            x_copies[4][0].start()
            x_copies[5][0].start()

        @pl.when(((part == 1) & (place == 3)) & (at == 13))
        def _():
            x_copies[0][1].start()
            x_copies[1][1].start()
            x_copies[2][1].start()
            x_copies[3][1].start()
            x_copies[4][1].start()
            x_copies[5][1].start()
            x_copies[0][0].start()
            x_copies[1][0].start()
            x_copies[2][0].start()
            x_copies[3][0].start()
            x_copies[4][0].start()
            x_copies[5][0].start()

    for load in loads[1:]:
        load.wait()

    def column(row):
        padded = jnp.concatenate([row, jnp.zeros((1, RPAD - RX), F32)], axis=1)
        turned = jnp.broadcast_to(padded, (BLOCK, RPAD)).T
        return turned[0:RROWS]

    for source, target in ((LP, LB), (AC, AB)):
        value = column(source[...].reshape(1, RX))
        target[:, 0:BLOCK] = value
        target[:, BLOCK:WIDE] = value

    def placed(value):
        wide = jnp.concatenate([value, jnp.zeros((SP, RPAD - RX), F32)], axis=1)
        return jnp.concatenate(
            [jnp.zeros((1, RPAD), F32), wide, jnp.zeros((CROWS - COMP, RPAD), F32)], axis=0
        )

    table = RT[...]
    first = placed(table[:, 0:RX])
    second = placed(table[:, RX : 2 * RX])
    for value, target in ((first, RA), (second, RB)):
        stacked = jnp.concatenate([value, value, value, jnp.zeros_like(value)], axis=0)
        target[...] = stacked.T[0:RROWS].astype(BF16)
    for k, value in enumerate((first, first, second, second)):
        C[:, k * RPAD : (k + 1) * RPAD] = value.astype(BF16)
    heat_row = jnp.concatenate([HT[...].reshape(1, RX), jnp.zeros((1, RPAD - RX), F32)], axis=1)
    heat_high, heat_mid, heat_low = split3(heat_row)
    row = lax.broadcasted_iota(jnp.int32, (CROWS, RPAD), 0)
    stoich = placed(PT[...])
    for at, piece in ((0, heat_high), (COMP, heat_mid), (COMP + 1, heat_low)):
        stoich = jnp.where(row == at, piece.astype(F32), stoich)
    PP[:, 0:RPAD] = stoich.astype(BF16)
    PP[:, RPAD : 2 * RPAD] = stoich.astype(BF16)
    Z[...] = jnp.zeros_like(Z)
    A[...] = jnp.zeros_like(A)

    before = jnp.zeros((8, BLOCK), jnp.int32)
    slot_plane = jnp.zeros((8, BLOCK), jnp.int32)
    slot_tile = jnp.zeros((8, BLOCK), jnp.int32) - 1
    slot_count = jnp.zeros((8, BLOCK), jnp.int32)
    burning = FL[...]
    counts = SB[...]
    for t in range(8):
        for x in range(8):
            lit = jnp.broadcast_to(burning[x : x + 1, t : t + 1], (8, BLOCK))
            steps = jnp.broadcast_to(counts[x : x + 1, t : t + 1], (8, BLOCK))
            match = (lit == 1) & (before == sub)
            slot_plane = jnp.where(match, x, slot_plane)
            slot_tile = jnp.where(match, t, slot_tile)
            slot_count = jnp.where(match, steps, slot_count)
            LV[t, x : x + 1, :] = lit[0:1]
            RK[t, x : x + 1, :] = jnp.minimum(before, SLOTS - 1)[0:1]
            before = before + lit
    step_size = 1.0 / jnp.maximum(slot_count, 1).astype(F32)
    for v in range(SLOTS):
        CN[:, v * BLOCK : (v + 1) * BLOCK] = jnp.broadcast_to(slot_count[v : v + 1], (8, BLOCK))
        ST[:, v * BLOCK : (v + 1) * BLOCK] = jnp.broadcast_to(step_size[v : v + 1], (8, BLOCK))

    def gather(c, _):
        value = jnp.zeros((8, BLOCK), F32) + 1.0
        for t in range(8):
            tile = S[c, :, t * BLOCK : (t + 1) * BLOCK]
            value = jnp.where(slot_tile == t, jnp.take_along_axis(tile, slot_plane, axis=0), value)
        Q[c] = value
        return 0

    looped(0, COMP, gather, 2)
    for v in range(SLOTS):
        A[0:COMP, v * BLOCK : (v + 1) * BLOCK] = Q[:, v, :]

    component = lax.broadcasted_iota(jnp.int32, (CROWS, WIDE), 0)

    def group(g, _):
        at = pl.ds(pl.multiple_of(g * WIDE, WIDE), WIDE)

        def substep(t, _):
            amounts = A[:, at]
            inverse = 1.0 / amounts[0:1]
            speeds = jnp.exp(LB[...] - AB[...] * inverse)
            pieces = split3(amounts)
            operand = jnp.concatenate([*pieces, jnp.zeros_like(pieces[0])], axis=0)
            first_side = jnp.dot(RA[...], operand, preferred_element_type=F32)
            second_side = jnp.dot(RB[...], operand, preferred_element_type=F32)
            to_first = speeds * second_side
            to_second = speeds * first_side
            progress = to_second * second_side
            for k, value in enumerate((to_first, to_second, progress)):
                high, low = split2(value)
                Z[2 * k * RPAD : 2 * k * RPAD + RROWS, :] = high
                Z[(2 * k + 1) * RPAD : (2 * k + 1) * RPAD + RROWS, :] = low
            consumed = jnp.dot(C[...], Z[0 : 4 * RPAD, :], preferred_element_type=F32)
            produced = jnp.dot(PP[...], Z[4 * RPAD : 6 * RPAD, :], preferred_element_type=F32)
            warmed = produced[0:1] + produced[COMP : COMP + 1] + produced[COMP + 1 : COMP + 2]
            produced = jnp.where(component == 0, warmed, produced)
            step = ST[0:1, at]
            updated = (amounts + step * produced) / (1.0 + step * consumed)
            checkpoint(1 + MAXSUB * g + t)
            active = (t < CN[0:1, at]) & (component < COMP)
            A[:, at] = jnp.where(active, updated, amounts)
            return 0

        lax.fori_loop(0, MAXSUB, substep, 0)
        return 0

    lax.fori_loop(0, SLOTS * BLOCK // WIDE, group, 0)
    for v in range(SLOTS):
        Q[:, v, :] = A[0:COMP, v * BLOCK : (v + 1) * BLOCK]

    zpos = lane % NZ

    def along_z(tile, offset):
        if offset > 0:
            return jnp.where(
                zpos < NZ - offset, pltpu.roll(tile, BLOCK - offset, 1), pltpu.roll(tile, NZ - offset, 1)
            )
        reach = -offset
        return jnp.where(zpos >= reach, pltpu.roll(tile, reach, 1), pltpu.roll(tile, BLOCK + reach - NZ, 1))

    def inner(c, _):
        checkpoint(17 + c)
        weight = DF[0, c]
        done = Q[c]
        tiles = [S[c, :, t * BLOCK : (t + 1) * BLOCK] for t in range(8)]
        plus = [pltpu.roll(x, BLOCK - NZ, 1) for x in tiles]
        minus = [pltpu.roll(x, NZ, 1) for x in tiles]
        half = [pltpu.roll(x, 2 * NZ, 1) for x in tiles]
        zero = jnp.zeros((8, BLOCK), F32)
        for t, x in enumerate(tiles):
            before_y = minus[t - 1] if t > 0 else zero
            after_y = plus[t + 1] if t < 7 else zero
            before_y2 = half[t - 1] if t > 0 else zero
            after_y2 = half[t + 1] if t < 7 else zero
            near = jnp.where(lane >= NZ, minus[t], before_y) + jnp.where(lane < BLOCK - NZ, plus[t], after_y)
            far = jnp.where(lane >= 2 * NZ, half[t], before_y2) + jnp.where(lane < 2 * NZ, half[t], after_y2)
            near = near + (along_z(x, 1) + along_z(x, -1))
            far = far + (along_z(x, 2) + along_z(x, -2))
            near = near + (
                jnp.where(sub >= 1, pltpu.roll(x, 1, 0), 0.0) + jnp.where(sub < 7, pltpu.roll(x, 7, 0), 0.0)
            )
            far = far + (
                jnp.where(sub >= 2, pltpu.roll(x, 2, 0), 0.0) + jnp.where(sub < 6, pltpu.roll(x, 6, 0), 0.0)
            )
            reacted = jnp.where(LV[t] == 1, jnp.take_along_axis(done, RK[t], axis=0), x)
            out[c, :, t * BLOCK : (t + 1) * BLOCK] = reacted + weight * (
                near_weight * near - far_weight * far - centre_weight * x
            )
        return 0

    looped(0, COMP, inner, 2)

    for copy in y_copies:
        copy.wait_recv()

    def edges(c, _):
        low, high = YR[0, c], YR[1, c]
        for comp, lo, hi in (
            (c, low, pltpu.roll(high, 64, 1)),
            (c + HALF, pltpu.roll(low, 64, 1), high),
        ):
            weight = DF[0, comp]
            near = jnp.where(lane < NZ, pltpu.roll(lo, BLOCK - NZ, 1), 0.0)
            far = jnp.where(lane < 2 * NZ, lo, 0.0)
            out[comp, :, 0:128] += weight * (near_weight * near - far_weight * far)
            near = jnp.where(lane >= BLOCK - NZ, pltpu.roll(hi, NZ, 1), 0.0)
            far = jnp.where(lane >= 2 * NZ, hi, 0.0)
            out[comp, :, 896:1024] += weight * (near_weight * near - far_weight * far)
        return 0

    looped(0, HALF, edges, 3)

    sub_row = lax.broadcasted_iota(jnp.int32, (8, 1024), 0)

    def outer(c, _):
        weight = DF[0, c]
        x = H[c]
        near = jnp.where(
            sub_row == 0, pltpu.roll(x, 1, 0), jnp.where(sub_row == 7, pltpu.roll(x, 7, 0), 0.0)
        )
        far = jnp.where(
            sub_row < 2, pltpu.roll(x, 2, 0), jnp.where(sub_row >= 6, pltpu.roll(x, 6, 0), 0.0)
        )
        out[c] += weight * (near_weight * near - far_weight * far)
        return 0

    for (c0, cn), pair in zip(CHUNKS, x_copies):
        for copy in pair:
            copy.wait_recv()
        looped(c0, cn, outer, 3)

    for pair in x_copies:
        for copy in pair:
            copy.wait_send()
    for copy in y_copies:
        copy.wait_send()


def per_device(
    state, diffusivity, log_prefactor, activation, heat, reactants, products, substeps, flame
):
    n, m = lax.axis_size("gx"), lax.axis_size("gy")
    anywhere = pl.BlockSpec(memory_space=pl.ANY)
    vmem, smem, dma = pltpu.VMEM, pltpu.SMEM, pltpu.SemaphoreType.DMA
    cells = state.shape[2]
    return pl.pallas_call(
        functools.partial(kernel, n, m),
        out_shape=pltpu.VMEM(state.shape, F32),
        in_specs=[anywhere] * 9,
        out_specs=pl.BlockSpec(memory_space=pltpu.VMEM),
        scratch_shapes=[
            vmem((COMP, 8, cells), F32),
            vmem((COMP, 8, cells), F32),
            vmem((2, HALF, 8, BLOCK), F32),
            vmem((2, HALF, 8, BLOCK), F32),
            smem((1, COMP), F32),
            vmem((RX,), F32),
            vmem((RX,), F32),
            vmem((RX,), F32),
            vmem((SP, 2 * RX), F32),
            vmem((SP, RX), F32),
            vmem((8, 8), jnp.int32),
            vmem((8, 8), jnp.int32),
            vmem((RROWS, WIDE), F32),
            vmem((RROWS, WIDE), F32),
            vmem((RROWS, 4 * CROWS), BF16),
            vmem((RROWS, 4 * CROWS), BF16),
            vmem((CROWS, 4 * RPAD), BF16),
            vmem((CROWS, 2 * RPAD), BF16),
            vmem((CROWS, SLOTS * BLOCK), F32),
            vmem((COMP, SLOTS, BLOCK), F32),
            vmem((8, SLOTS * BLOCK), jnp.int32),
            vmem((8, SLOTS * BLOCK), F32),
            vmem((6 * RPAD, WIDE), BF16),
            vmem((8, 8, BLOCK), jnp.int32),
            vmem((8, 8, BLOCK), jnp.int32),
            dma((2, len(CHUNKS))), dma((2, len(CHUNKS))), dma((2,)), dma((2,)), dma((9,)),
        ],
        compiler_params=pltpu.CompilerParams(
            collective_id=0, has_side_effects=True, vmem_limit_bytes=VMEM_LIMIT
        ),
    )(
        state, diffusivity.reshape(1, -1), log_prefactor, activation,
        heat, reactants.T, products, substeps, flame,
    )


VMEM_LIMIT = 60 << 20


def solution(mesh):
    in_specs = (P(None, "gx", "gy"), P(), P(), P(), P(), P(), P(), P("gx", "gy"), P("gx", "gy"))
    return jax.shard_map(
        per_device, mesh=mesh, in_specs=in_specs, out_specs=P(None, "gx", "gy"), check_vma=False
    )
```

```python
import functools

import jax
import jax.numpy as jnp
from jax import lax
from jax.experimental import pallas as pl
from jax.experimental.pallas import tpu as pltpu
from jax.sharding import PartitionSpec as P

NZ = 32
BLOCK = 128
MAXSUB = 4
SLOTS = 8
SP = 53
COMP = 54
RX = 325
CROWS = 64
RROWS = 336
RPAD = 384
WIDE = 256
HALF = COMP // 2
CHUNKS = ((0, 9), (9, 9), (18, 9), (27, 9), (36, 9), (45, 9))

near_weight = 4.0 / 3.0
far_weight = 1.0 / 12.0
centre_weight = 7.5

MESH = pl.DeviceIdType.MESH
F32 = jnp.float32
BF16 = jnp.bfloat16


def split2(x):
    high = x.astype(BF16)
    return high, (x - high.astype(F32)).astype(BF16)


def split3(x):
    high = x.astype(BF16)
    rest = x - high.astype(F32)
    middle = rest.astype(BF16)
    return high, middle, (rest - middle.astype(F32)).astype(BF16)


def looped(first, count, body, together):
    def step(i, _):
        for k in range(together):
            body(first + i * together + k, 0)
        return 0

    lax.fori_loop(0, count // together, step, 0)


def kernel(
    n, m,
    state, diffusivity, log_prefactor, activation, heat, reactants_t, products, substeps, flame,
    out,
    S, H, YS, YR, DF, LP, AC, HT, RT, PT, SB, FL,
    LB, AB, RA, RB, C, PP, A, Q, CN, ST, Z, LV, RK,
    x_send, x_recv, y_send, y_recv, local, from_right, from_left, from_up, from_down,
):
    gx, gy = lax.axis_index("gx"), lax.axis_index("gy")
    right, left = lax.rem(gx + 1, n), lax.rem(gx + n - 1, n)
    up, down = lax.rem(gy + 1, m), lax.rem(gy + m - 1, m)

    barrier = pltpu.get_barrier_semaphore()
    part = lax.rem(gx, 3)
    place = gy // 2

    def tell(semaphore, device):
        pl.semaphore_signal(semaphore, inc=1, device_id=device, device_id_type=MESH)

    @pl.when(part == 0)
    def _():
        tell(barrier, (right, gy))
        tell(barrier, (left, gy))

    @pl.when(part == 1)
    def _():
        tell(barrier, (right, gy))

    @pl.when(gy < m - 1)
    def _():
        tell(barrier, (gx, up))

    @pl.when(gy == 0)
    def _():
        tell(barrier, (gx, down))


    loads = [
        pltpu.make_async_copy(state, S, local.at[0]),
        pltpu.make_async_copy(diffusivity, DF, local.at[1]),
        pltpu.make_async_copy(log_prefactor, LP, local.at[2]),
        pltpu.make_async_copy(activation, AC, local.at[3]),
        pltpu.make_async_copy(heat, HT, local.at[4]),
        pltpu.make_async_copy(reactants_t, RT, local.at[5]),
        pltpu.make_async_copy(products, PT, local.at[6]),
        pltpu.make_async_copy(substeps, SB, local.at[7]),
        pltpu.make_async_copy(flame, FL, local.at[8]),
    ]
    for load in loads:
        load.start()

    @pl.when(part + gy > 0)
    def _():
        pl.semaphore_wait(barrier, part + (gy + m - 2) // (m - 1) + gy // (m - 1))

    @pl.when(part >= 1)
    def _():
        tell(from_right, (left, gy))

    @pl.when(part == 2)
    def _():
        tell(from_left, (right, gy))

    @pl.when(gy >= 1)
    def _():
        tell(from_up, (gx, down))

    @pl.when(gy == m - 1)
    def _():
        tell(from_down, (gx, up))

    x_copies = []
    for k, (c0, cn) in enumerate(CHUNKS):
        pair = (
            pltpu.make_async_remote_copy(
                state.at[c0 : c0 + cn, 6:8, :], H.at[c0 : c0 + cn, 6:8, :],
                x_send.at[0, k], x_recv.at[0, k], device_id=(right, gy), device_id_type=MESH,
            ),
            pltpu.make_async_remote_copy(
                state.at[c0 : c0 + cn, 0:2, :], H.at[c0 : c0 + cn, 0:2, :],
                x_send.at[1, k], x_recv.at[1, k], device_id=(left, gy), device_id_type=MESH,
            ),
        )
        x_copies.append(pair)

    @pl.when(part == 2)
    def _():
        x_copies[0][0].start()
        x_copies[1][0].start()
        x_copies[0][1].start()

    @pl.when(part == 1)
    def _():
        x_copies[0][1].start()
        x_copies[1][1].start()

    loads[0].wait()
    lane = lax.broadcasted_iota(jnp.int32, (8, BLOCK), 1)
    sub = lax.broadcasted_iota(jnp.int32, (8, BLOCK), 0)

    def pack(c, _):
        YS[0, c] = jnp.where(
            lane < 64,
            pltpu.roll(S[c, :, 896:1024], 64, 1),
            S[c + HALF, :, 896:1024],
        )
        YS[1, c] = jnp.where(
            lane < 64,
            S[c, :, 0:128],
            pltpu.roll(S[c + HALF, :, 0:128], 64, 1),
        )
        return 0

    looped(0, HALF, pack, 3)

    y_copies = [
        pltpu.make_async_remote_copy(
            YS.at[0], YR.at[0], y_send.at[0], y_recv.at[0], device_id=(gx, up), device_id_type=MESH
        ),
        pltpu.make_async_remote_copy(
            YS.at[1], YR.at[1], y_send.at[1], y_recv.at[1], device_id=(gx, down), device_id_type=MESH
        ),
    ]
    @pl.when(gy >= 1)
    def _():
        y_copies[1].start()

    @pl.when(gy == m - 1)
    def _():
        y_copies[0].start()

    @pl.when(part == 2)
    def _():
        x_copies[2][0].start()
        x_copies[1][1].start()
        x_copies[3][0].start()
        x_copies[2][1].start()
        x_copies[4][0].start()
        x_copies[3][1].start()
        x_copies[5][0].start()
        x_copies[4][1].start()
        x_copies[5][1].start()

    @pl.when(part == 1)
    def _():
        x_copies[2][1].start()
        x_copies[3][1].start()
        x_copies[4][1].start()
        x_copies[5][1].start()

    @pl.when(gy < m - 1)
    def _():
        pl.semaphore_wait(from_up, 1)
        y_copies[0].start()

    @pl.when(gy == 0)
    def _():
        pl.semaphore_wait(from_down, 1)
        y_copies[1].start()

    @pl.when(part <= 1)
    def _():
        pl.semaphore_wait(from_right, 1)

    @pl.when(part == 0)
    def _():
        x_copies[0][0].start()
        x_copies[1][0].start()
        x_copies[2][0].start()
        x_copies[3][0].start()
        x_copies[4][0].start()
        x_copies[5][0].start()

    @pl.when(part == 1)
    def _():
        x_copies[0][0].start()
        x_copies[1][0].start()
        x_copies[2][0].start()
        x_copies[3][0].start()
        x_copies[4][0].start()
        x_copies[5][0].start()

    @pl.when(part == 0)
    def _():
        pl.semaphore_wait(from_left, 1)

    @pl.when(part == 0)
    def _():
        x_copies[0][1].start()
        x_copies[1][1].start()
        x_copies[2][1].start()
        x_copies[3][1].start()
        x_copies[4][1].start()
        x_copies[5][1].start()

    for load in loads[1:]:
        load.wait()

    def column(row):
        padded = jnp.concatenate([row, jnp.zeros((1, RPAD - RX), F32)], axis=1)
        turned = jnp.broadcast_to(padded, (BLOCK, RPAD)).T
        return turned[0:RROWS]

    for source, target in ((LP, LB), (AC, AB)):
        value = column(source[...].reshape(1, RX))
        target[:, 0:BLOCK] = value
        target[:, BLOCK:WIDE] = value

    def placed(value):
        wide = jnp.concatenate([value, jnp.zeros((SP, RPAD - RX), F32)], axis=1)
        return jnp.concatenate(
            [jnp.zeros((1, RPAD), F32), wide, jnp.zeros((CROWS - COMP, RPAD), F32)], axis=0
        )

    table = RT[...]
    first = placed(table[:, 0:RX])
    second = placed(table[:, RX : 2 * RX])
    for value, target in ((first, RA), (second, RB)):
        stacked = jnp.concatenate([value, value, value, jnp.zeros_like(value)], axis=0)
        target[...] = stacked.T[0:RROWS].astype(BF16)
    for k, value in enumerate((first, first, second, second)):
        C[:, k * RPAD : (k + 1) * RPAD] = value.astype(BF16)
    heat_row = jnp.concatenate([HT[...].reshape(1, RX), jnp.zeros((1, RPAD - RX), F32)], axis=1)
    heat_high, heat_mid, heat_low = split3(heat_row)
    row = lax.broadcasted_iota(jnp.int32, (CROWS, RPAD), 0)
    stoich = placed(PT[...])
    for at, piece in ((0, heat_high), (COMP, heat_mid), (COMP + 1, heat_low)):
        stoich = jnp.where(row == at, piece.astype(F32), stoich)
    PP[:, 0:RPAD] = stoich.astype(BF16)
    PP[:, RPAD : 2 * RPAD] = stoich.astype(BF16)
    Z[...] = jnp.zeros_like(Z)
    A[...] = jnp.zeros_like(A)

    before = jnp.zeros((8, BLOCK), jnp.int32)
    slot_plane = jnp.zeros((8, BLOCK), jnp.int32)
    slot_tile = jnp.zeros((8, BLOCK), jnp.int32) - 1
    slot_count = jnp.zeros((8, BLOCK), jnp.int32)
    burning = FL[...]
    counts = SB[...]
    for t in range(8):
        for x in range(8):
            lit = jnp.broadcast_to(burning[x : x + 1, t : t + 1], (8, BLOCK))
            steps = jnp.broadcast_to(counts[x : x + 1, t : t + 1], (8, BLOCK))
            match = (lit == 1) & (before == sub)
            slot_plane = jnp.where(match, x, slot_plane)
            slot_tile = jnp.where(match, t, slot_tile)
            slot_count = jnp.where(match, steps, slot_count)
            LV[t, x : x + 1, :] = lit[0:1]
            RK[t, x : x + 1, :] = jnp.minimum(before, SLOTS - 1)[0:1]
            before = before + lit
    step_size = 1.0 / jnp.maximum(slot_count, 1).astype(F32)
    for v in range(SLOTS):
        CN[:, v * BLOCK : (v + 1) * BLOCK] = jnp.broadcast_to(slot_count[v : v + 1], (8, BLOCK))
        ST[:, v * BLOCK : (v + 1) * BLOCK] = jnp.broadcast_to(step_size[v : v + 1], (8, BLOCK))

    def gather(c, _):
        value = jnp.zeros((8, BLOCK), F32) + 1.0
        for t in range(8):
            tile = S[c, :, t * BLOCK : (t + 1) * BLOCK]
            value = jnp.where(slot_tile == t, jnp.take_along_axis(tile, slot_plane, axis=0), value)
        Q[c] = value
        return 0

    looped(0, COMP, gather, 2)
    for v in range(SLOTS):
        A[0:COMP, v * BLOCK : (v + 1) * BLOCK] = Q[:, v, :]

    component = lax.broadcasted_iota(jnp.int32, (CROWS, WIDE), 0)

    def group(g, _):
        at = pl.ds(pl.multiple_of(g * WIDE, WIDE), WIDE)

        def substep(t, _):
            amounts = A[:, at]
            inverse = 1.0 / amounts[0:1]
            speeds = jnp.exp(LB[...] - AB[...] * inverse)
            pieces = split3(amounts)
            operand = jnp.concatenate([*pieces, jnp.zeros_like(pieces[0])], axis=0)
            first_side = jnp.dot(RA[...], operand, preferred_element_type=F32)
            second_side = jnp.dot(RB[...], operand, preferred_element_type=F32)
            to_first = speeds * second_side
            to_second = speeds * first_side
            progress = to_second * second_side
            for k, value in enumerate((to_first, to_second, progress)):
                high, low = split2(value)
                Z[2 * k * RPAD : 2 * k * RPAD + RROWS, :] = high
                Z[(2 * k + 1) * RPAD : (2 * k + 1) * RPAD + RROWS, :] = low
            consumed = jnp.dot(C[...], Z[0 : 4 * RPAD, :], preferred_element_type=F32)
            produced = jnp.dot(PP[...], Z[4 * RPAD : 6 * RPAD, :], preferred_element_type=F32)
            warmed = produced[0:1] + produced[COMP : COMP + 1] + produced[COMP + 1 : COMP + 2]
            produced = jnp.where(component == 0, warmed, produced)
            step = ST[0:1, at]
            updated = (amounts + step * produced) / (1.0 + step * consumed)
            active = (t < CN[0:1, at]) & (component < COMP)
            A[:, at] = jnp.where(active, updated, amounts)
            return 0

        lax.fori_loop(0, MAXSUB, substep, 0)
        return 0

    lax.fori_loop(0, SLOTS * BLOCK // WIDE, group, 0)
    for v in range(SLOTS):
        Q[:, v, :] = A[0:COMP, v * BLOCK : (v + 1) * BLOCK]

    zpos = lane % NZ

    def along_z(tile, offset):
        if offset > 0:
            return jnp.where(
                zpos < NZ - offset, pltpu.roll(tile, BLOCK - offset, 1), pltpu.roll(tile, NZ - offset, 1)
            )
        reach = -offset
        return jnp.where(zpos >= reach, pltpu.roll(tile, reach, 1), pltpu.roll(tile, BLOCK + reach - NZ, 1))

    def inner(c, _):
        weight = DF[0, c]
        done = Q[c]
        tiles = [S[c, :, t * BLOCK : (t + 1) * BLOCK] for t in range(8)]
        plus = [pltpu.roll(x, BLOCK - NZ, 1) for x in tiles]
        minus = [pltpu.roll(x, NZ, 1) for x in tiles]
        half = [pltpu.roll(x, 2 * NZ, 1) for x in tiles]
        zero = jnp.zeros((8, BLOCK), F32)
        for t, x in enumerate(tiles):
            before_y = minus[t - 1] if t > 0 else zero
            after_y = plus[t + 1] if t < 7 else zero
            before_y2 = half[t - 1] if t > 0 else zero
            after_y2 = half[t + 1] if t < 7 else zero
            near = jnp.where(lane >= NZ, minus[t], before_y) + jnp.where(lane < BLOCK - NZ, plus[t], after_y)
            far = jnp.where(lane >= 2 * NZ, half[t], before_y2) + jnp.where(lane < 2 * NZ, half[t], after_y2)
            near = near + (along_z(x, 1) + along_z(x, -1))
            far = far + (along_z(x, 2) + along_z(x, -2))
            near = near + (
                jnp.where(sub >= 1, pltpu.roll(x, 1, 0), 0.0) + jnp.where(sub < 7, pltpu.roll(x, 7, 0), 0.0)
            )
            far = far + (
                jnp.where(sub >= 2, pltpu.roll(x, 2, 0), 0.0) + jnp.where(sub < 6, pltpu.roll(x, 6, 0), 0.0)
            )
            reacted = jnp.where(LV[t] == 1, jnp.take_along_axis(done, RK[t], axis=0), x)
            out[c, :, t * BLOCK : (t + 1) * BLOCK] = reacted + weight * (
                near_weight * near - far_weight * far - centre_weight * x
            )
        return 0

    looped(0, COMP, inner, 2)

    for copy in y_copies:
        copy.wait_recv()

    def edges(c, _):
        low, high = YR[0, c], YR[1, c]
        for comp, lo, hi in (
            (c, low, pltpu.roll(high, 64, 1)),
            (c + HALF, pltpu.roll(low, 64, 1), high),
        ):
            weight = DF[0, comp]
            near = jnp.where(lane < NZ, pltpu.roll(lo, BLOCK - NZ, 1), 0.0)
            far = jnp.where(lane < 2 * NZ, lo, 0.0)
            out[comp, :, 0:128] += weight * (near_weight * near - far_weight * far)
            near = jnp.where(lane >= BLOCK - NZ, pltpu.roll(hi, NZ, 1), 0.0)
            far = jnp.where(lane >= 2 * NZ, hi, 0.0)
            out[comp, :, 896:1024] += weight * (near_weight * near - far_weight * far)
        return 0

    looped(0, HALF, edges, 3)

    sub_row = lax.broadcasted_iota(jnp.int32, (8, 1024), 0)

    def outer(c, _):
        weight = DF[0, c]
        x = H[c]
        near = jnp.where(
            sub_row == 0, pltpu.roll(x, 1, 0), jnp.where(sub_row == 7, pltpu.roll(x, 7, 0), 0.0)
        )
        far = jnp.where(
            sub_row < 2, pltpu.roll(x, 2, 0), jnp.where(sub_row >= 6, pltpu.roll(x, 6, 0), 0.0)
        )
        out[c] += weight * (near_weight * near - far_weight * far)
        return 0

    for (c0, cn), pair in zip(CHUNKS, x_copies):
        for copy in pair:
            copy.wait_recv()
        looped(c0, cn, outer, 3)

    for pair in x_copies:
        for copy in pair:
            copy.wait_send()
    for copy in y_copies:
        copy.wait_send()


def per_device(
    state, diffusivity, log_prefactor, activation, heat, reactants, products, substeps, flame
):
    n, m = lax.axis_size("gx"), lax.axis_size("gy")
    anywhere = pl.BlockSpec(memory_space=pl.ANY)
    vmem, smem, dma = pltpu.VMEM, pltpu.SMEM, pltpu.SemaphoreType.DMA
    cells = state.shape[2]
    return pl.pallas_call(
        functools.partial(kernel, n, m),
        out_shape=pltpu.VMEM(state.shape, F32),
        in_specs=[anywhere] * 9,
        out_specs=pl.BlockSpec(memory_space=pltpu.VMEM),
        scratch_shapes=[
            vmem((COMP, 8, cells), F32),
            vmem((COMP, 8, cells), F32),
            vmem((2, HALF, 8, BLOCK), F32),
            vmem((2, HALF, 8, BLOCK), F32),
            smem((1, COMP), F32),
            vmem((RX,), F32),
            vmem((RX,), F32),
            vmem((RX,), F32),
            vmem((SP, 2 * RX), F32),
            vmem((SP, RX), F32),
            vmem((8, 8), jnp.int32),
            vmem((8, 8), jnp.int32),
            vmem((RROWS, WIDE), F32),
            vmem((RROWS, WIDE), F32),
            vmem((RROWS, 4 * CROWS), BF16),
            vmem((RROWS, 4 * CROWS), BF16),
            vmem((CROWS, 4 * RPAD), BF16),
            vmem((CROWS, 2 * RPAD), BF16),
            vmem((CROWS, SLOTS * BLOCK), F32),
            vmem((COMP, SLOTS, BLOCK), F32),
            vmem((8, SLOTS * BLOCK), jnp.int32),
            vmem((8, SLOTS * BLOCK), F32),
            vmem((6 * RPAD, WIDE), BF16),
            vmem((8, 8, BLOCK), jnp.int32),
            vmem((8, 8, BLOCK), jnp.int32),
            dma((2, len(CHUNKS))), dma((2, len(CHUNKS))), dma((2,)), dma((2,)), dma((9,)),
            *[pltpu.SemaphoreType.REGULAR] * 4,
        ],
        compiler_params=pltpu.CompilerParams(
            collective_id=0, has_side_effects=True, vmem_limit_bytes=VMEM_LIMIT
        ),
    )(
        state, diffusivity.reshape(1, -1), log_prefactor, activation,
        heat, reactants.T, products, substeps, flame,
    )


VMEM_LIMIT = 60 << 20


def solution(mesh):
    in_specs = (P(None, "gx", "gy"), P(), P(), P(), P(), P(), P(), P("gx", "gy"), P("gx", "gy"))
    return jax.shard_map(
        per_device, mesh=mesh, in_specs=in_specs, out_specs=P(None, "gx", "gy"), check_vma=False
    )
```

```python
import functools

import jax
import jax.numpy as jnp
from jax import lax
from jax.experimental import pallas as pl
from jax.experimental.pallas import tpu as pltpu
from jax.sharding import PartitionSpec as P

NZ = 32
BLOCK = 128
MAXSUB = 4
SLOTS = 8
SP = 53
COMP = 54
RX = 325
CROWS = 64
RROWS = 336
RPAD = 384
WIDE = 256
HALF = COMP // 2
CHUNKS = ((0, 12), (12, 12), (24, 12), (36, 9), (45, 6), (51, 3))

near_weight = 4.0 / 3.0
far_weight = 1.0 / 12.0
centre_weight = 7.5

MESH = pl.DeviceIdType.MESH
F32 = jnp.float32
BF16 = jnp.bfloat16


def split2(x):
    high = x.astype(BF16)
    return high, (x - high.astype(F32)).astype(BF16)


def split3(x):
    high = x.astype(BF16)
    rest = x - high.astype(F32)
    middle = rest.astype(BF16)
    return high, middle, (rest - middle.astype(F32)).astype(BF16)


def looped(first, count, body, together):
    def step(i, _):
        for k in range(together):
            body(first + i * together + k, 0)
        return 0

    lax.fori_loop(0, count // together, step, 0)


def kernel(
    n, m,
    state, diffusivity, log_prefactor, activation, heat, reactants_t, products, substeps, flame,
    out,
    S, H, YS, YR, DF, LP, AC, HT, RT, PT, SB, FL,
    LB, AB, RA, RB, C, PP, A, Q, CN, ST, Z, LV, RK,
    x_send, x_recv, y_send, y_recv, local, from_right, from_left, from_up, from_down,
):
    gx, gy = lax.axis_index("gx"), lax.axis_index("gy")
    right, left = lax.rem(gx + 1, n), lax.rem(gx + n - 1, n)
    up, down = lax.rem(gy + 1, m), lax.rem(gy + m - 1, m)

    barrier = pltpu.get_barrier_semaphore()
    part = lax.rem(gx, 3)
    place = gy // 2

    def tell(semaphore, device):
        pl.semaphore_signal(semaphore, inc=1, device_id=device, device_id_type=MESH)

    @pl.when(part == 0)
    def _():
        tell(barrier, (right, gy))
        tell(barrier, (left, gy))

    @pl.when(part == 1)
    def _():
        tell(barrier, (right, gy))

    @pl.when(gy < m - 1)
    def _():
        tell(barrier, (gx, up))

    @pl.when(gy == 0)
    def _():
        tell(barrier, (gx, down))


    @pl.when(part + gy > 0)
    def _():
        pl.semaphore_wait(barrier, part + (gy + m - 2) // (m - 1) + gy // (m - 1))

    @pl.when(part >= 1)
    def _():
        tell(from_right, (left, gy))

    @pl.when(part == 2)
    def _():
        tell(from_left, (right, gy))

    @pl.when(gy >= 1)
    def _():
        tell(from_up, (gx, down))

    @pl.when(gy == m - 1)
    def _():
        tell(from_down, (gx, up))

    x_copies = []
    for k, (c0, cn) in enumerate(CHUNKS):
        pair = (
            pltpu.make_async_remote_copy(
                state.at[c0 : c0 + cn, 6:8, :], H.at[c0 : c0 + cn, 6:8, :],
                x_send.at[0, k], x_recv.at[0, k], device_id=(right, gy), device_id_type=MESH,
            ),
            pltpu.make_async_remote_copy(
                state.at[c0 : c0 + cn, 0:2, :], H.at[c0 : c0 + cn, 0:2, :],
                x_send.at[1, k], x_recv.at[1, k], device_id=(left, gy), device_id_type=MESH,
            ),
        )
        x_copies.append(pair)

    @pl.when(part == 2)
    def _():
        x_copies[0][0].start()
        x_copies[1][0].start()
        x_copies[2][0].start()
        x_copies[3][0].start()
        x_copies[4][0].start()
        x_copies[5][0].start()
        x_copies[0][1].start()

    @pl.when(part == 1)
    def _():
        x_copies[0][1].start()
        x_copies[1][1].start()
        x_copies[2][1].start()
        x_copies[3][1].start()
        x_copies[4][1].start()
        x_copies[5][1].start()

    loads = [
        pltpu.make_async_copy(state, S, local.at[0]),
        pltpu.make_async_copy(diffusivity, DF, local.at[1]),
        pltpu.make_async_copy(log_prefactor, LP, local.at[2]),
        pltpu.make_async_copy(activation, AC, local.at[3]),
        pltpu.make_async_copy(heat, HT, local.at[4]),
        pltpu.make_async_copy(reactants_t, RT, local.at[5]),
        pltpu.make_async_copy(products, PT, local.at[6]),
        pltpu.make_async_copy(substeps, SB, local.at[7]),
        pltpu.make_async_copy(flame, FL, local.at[8]),
    ]
    for load in loads:
        load.start()

    loads[0].wait()
    lane = lax.broadcasted_iota(jnp.int32, (8, BLOCK), 1)
    sub = lax.broadcasted_iota(jnp.int32, (8, BLOCK), 0)

    def pack(c, _):
        YS[0, c] = jnp.where(
            lane < 64,
            pltpu.roll(S[c, :, 896:1024], 64, 1),
            S[c + HALF, :, 896:1024],
        )
        YS[1, c] = jnp.where(
            lane < 64,
            S[c, :, 0:128],
            pltpu.roll(S[c + HALF, :, 0:128], 64, 1),
        )
        return 0

    looped(0, HALF, pack, 3)

    y_copies = [
        pltpu.make_async_remote_copy(
            YS.at[0], YR.at[0], y_send.at[0], y_recv.at[0], device_id=(gx, up), device_id_type=MESH
        ),
        pltpu.make_async_remote_copy(
            YS.at[1], YR.at[1], y_send.at[1], y_recv.at[1], device_id=(gx, down), device_id_type=MESH
        ),
    ]
    @pl.when(gy >= 1)
    def _():
        y_copies[1].start()

    @pl.when(gy == m - 1)
    def _():
        y_copies[0].start()

    @pl.when(part == 2)
    def _():
        x_copies[1][1].start()
        x_copies[2][1].start()
        x_copies[3][1].start()
        x_copies[4][1].start()
        x_copies[5][1].start()

    @pl.when(gy < m - 1)
    def _():
        pl.semaphore_wait(from_up, 1)
        y_copies[0].start()

    @pl.when(gy == 0)
    def _():
        pl.semaphore_wait(from_down, 1)
        y_copies[1].start()

    @pl.when(part <= 1)
    def _():
        pl.semaphore_wait(from_right, 1)

    @pl.when(part == 0)
    def _():
        x_copies[0][0].start()
        x_copies[1][0].start()
        x_copies[2][0].start()
        x_copies[3][0].start()
        x_copies[4][0].start()
        x_copies[5][0].start()

    @pl.when(part == 1)
    def _():
        x_copies[0][0].start()
        x_copies[1][0].start()
        x_copies[2][0].start()
        x_copies[3][0].start()
        x_copies[4][0].start()
        x_copies[5][0].start()

    @pl.when(part == 0)
    def _():
        pl.semaphore_wait(from_left, 1)

    @pl.when(part == 0)
    def _():
        x_copies[0][1].start()
        x_copies[1][1].start()
        x_copies[2][1].start()
        x_copies[3][1].start()
        x_copies[4][1].start()
        x_copies[5][1].start()

    for load in loads[1:]:
        load.wait()

    def column(row):
        padded = jnp.concatenate([row, jnp.zeros((1, RPAD - RX), F32)], axis=1)
        turned = jnp.broadcast_to(padded, (BLOCK, RPAD)).T
        return turned[0:RROWS]

    for source, target in ((LP, LB), (AC, AB)):
        value = column(source[...].reshape(1, RX))
        target[:, 0:BLOCK] = value
        target[:, BLOCK:WIDE] = value

    def placed(value):
        wide = jnp.concatenate([value, jnp.zeros((SP, RPAD - RX), F32)], axis=1)
        return jnp.concatenate(
            [jnp.zeros((1, RPAD), F32), wide, jnp.zeros((CROWS - COMP, RPAD), F32)], axis=0
        )

    table = RT[...]
    first = placed(table[:, 0:RX])
    second = placed(table[:, RX : 2 * RX])
    for value, target in ((first, RA), (second, RB)):
        stacked = jnp.concatenate([value, value, value, jnp.zeros_like(value)], axis=0)
        target[...] = stacked.T[0:RROWS].astype(BF16)
    for k, value in enumerate((first, first, second, second)):
        C[:, k * RPAD : (k + 1) * RPAD] = value.astype(BF16)
    heat_row = jnp.concatenate([HT[...].reshape(1, RX), jnp.zeros((1, RPAD - RX), F32)], axis=1)
    heat_high, heat_mid, heat_low = split3(heat_row)
    row = lax.broadcasted_iota(jnp.int32, (CROWS, RPAD), 0)
    stoich = placed(PT[...])
    for at, piece in ((0, heat_high), (COMP, heat_mid), (COMP + 1, heat_low)):
        stoich = jnp.where(row == at, piece.astype(F32), stoich)
    PP[:, 0:RPAD] = stoich.astype(BF16)
    PP[:, RPAD : 2 * RPAD] = stoich.astype(BF16)
    Z[...] = jnp.zeros_like(Z)
    A[...] = jnp.zeros_like(A)

    before = jnp.zeros((8, BLOCK), jnp.int32)
    slot_plane = jnp.zeros((8, BLOCK), jnp.int32)
    slot_tile = jnp.zeros((8, BLOCK), jnp.int32) - 1
    slot_count = jnp.zeros((8, BLOCK), jnp.int32)
    burning = FL[...]
    counts = SB[...]
    for t in range(8):
        for x in range(8):
            lit = jnp.broadcast_to(burning[x : x + 1, t : t + 1], (8, BLOCK))
            steps = jnp.broadcast_to(counts[x : x + 1, t : t + 1], (8, BLOCK))
            match = (lit == 1) & (before == sub)
            slot_plane = jnp.where(match, x, slot_plane)
            slot_tile = jnp.where(match, t, slot_tile)
            slot_count = jnp.where(match, steps, slot_count)
            LV[t, x : x + 1, :] = lit[0:1]
            RK[t, x : x + 1, :] = jnp.minimum(before, SLOTS - 1)[0:1]
            before = before + lit
    step_size = 1.0 / jnp.maximum(slot_count, 1).astype(F32)
    for v in range(SLOTS):
        CN[:, v * BLOCK : (v + 1) * BLOCK] = jnp.broadcast_to(slot_count[v : v + 1], (8, BLOCK))
        ST[:, v * BLOCK : (v + 1) * BLOCK] = jnp.broadcast_to(step_size[v : v + 1], (8, BLOCK))

    def gather(c, _):
        value = jnp.zeros((8, BLOCK), F32) + 1.0
        for t in range(8):
            tile = S[c, :, t * BLOCK : (t + 1) * BLOCK]
            value = jnp.where(slot_tile == t, jnp.take_along_axis(tile, slot_plane, axis=0), value)
        Q[c] = value
        return 0

    looped(0, COMP, gather, 2)
    for v in range(SLOTS):
        A[0:COMP, v * BLOCK : (v + 1) * BLOCK] = Q[:, v, :]

    component = lax.broadcasted_iota(jnp.int32, (CROWS, WIDE), 0)

    def group(g, _):
        at = pl.ds(pl.multiple_of(g * WIDE, WIDE), WIDE)

        def substep(t, _):
            amounts = A[:, at]
            inverse = 1.0 / amounts[0:1]
            speeds = jnp.exp(LB[...] - AB[...] * inverse)
            pieces = split3(amounts)
            operand = jnp.concatenate([*pieces, jnp.zeros_like(pieces[0])], axis=0)
            first_side = jnp.dot(RA[...], operand, preferred_element_type=F32)
            second_side = jnp.dot(RB[...], operand, preferred_element_type=F32)
            to_first = speeds * second_side
            to_second = speeds * first_side
            progress = to_second * second_side
            for k, value in enumerate((to_first, to_second, progress)):
                high, low = split2(value)
                Z[2 * k * RPAD : 2 * k * RPAD + RROWS, :] = high
                Z[(2 * k + 1) * RPAD : (2 * k + 1) * RPAD + RROWS, :] = low
            consumed = jnp.dot(C[...], Z[0 : 4 * RPAD, :], preferred_element_type=F32)
            produced = jnp.dot(PP[...], Z[4 * RPAD : 6 * RPAD, :], preferred_element_type=F32)
            warmed = produced[0:1] + produced[COMP : COMP + 1] + produced[COMP + 1 : COMP + 2]
            produced = jnp.where(component == 0, warmed, produced)
            step = ST[0:1, at]
            updated = (amounts + step * produced) / (1.0 + step * consumed)
            active = (t < CN[0:1, at]) & (component < COMP)
            A[:, at] = jnp.where(active, updated, amounts)
            return 0

        lax.fori_loop(0, MAXSUB, substep, 0)
        return 0

    lax.fori_loop(0, SLOTS * BLOCK // WIDE, group, 0)
    for v in range(SLOTS):
        Q[:, v, :] = A[0:COMP, v * BLOCK : (v + 1) * BLOCK]

    zpos = lane % NZ

    def along_z(tile, offset):
        if offset > 0:
            return jnp.where(
                zpos < NZ - offset, pltpu.roll(tile, BLOCK - offset, 1), pltpu.roll(tile, NZ - offset, 1)
            )
        reach = -offset
        return jnp.where(zpos >= reach, pltpu.roll(tile, reach, 1), pltpu.roll(tile, BLOCK + reach - NZ, 1))

    def inner(c, _):
        weight = DF[0, c]
        done = Q[c]
        tiles = [S[c, :, t * BLOCK : (t + 1) * BLOCK] for t in range(8)]
        plus = [pltpu.roll(x, BLOCK - NZ, 1) for x in tiles]
        minus = [pltpu.roll(x, NZ, 1) for x in tiles]
        half = [pltpu.roll(x, 2 * NZ, 1) for x in tiles]
        zero = jnp.zeros((8, BLOCK), F32)
        for t, x in enumerate(tiles):
            before_y = minus[t - 1] if t > 0 else zero
            after_y = plus[t + 1] if t < 7 else zero
            before_y2 = half[t - 1] if t > 0 else zero
            after_y2 = half[t + 1] if t < 7 else zero
            near = jnp.where(lane >= NZ, minus[t], before_y) + jnp.where(lane < BLOCK - NZ, plus[t], after_y)
            far = jnp.where(lane >= 2 * NZ, half[t], before_y2) + jnp.where(lane < 2 * NZ, half[t], after_y2)
            near = near + (along_z(x, 1) + along_z(x, -1))
            far = far + (along_z(x, 2) + along_z(x, -2))
            near = near + (
                jnp.where(sub >= 1, pltpu.roll(x, 1, 0), 0.0) + jnp.where(sub < 7, pltpu.roll(x, 7, 0), 0.0)
            )
            far = far + (
                jnp.where(sub >= 2, pltpu.roll(x, 2, 0), 0.0) + jnp.where(sub < 6, pltpu.roll(x, 6, 0), 0.0)
            )
            reacted = jnp.where(LV[t] == 1, jnp.take_along_axis(done, RK[t], axis=0), x)
            out[c, :, t * BLOCK : (t + 1) * BLOCK] = reacted + weight * (
                near_weight * near - far_weight * far - centre_weight * x
            )
        return 0

    looped(0, COMP, inner, 2)

    for copy in y_copies:
        copy.wait_recv()

    def edges(c, _):
        low, high = YR[0, c], YR[1, c]
        for comp, lo, hi in (
            (c, low, pltpu.roll(high, 64, 1)),
            (c + HALF, pltpu.roll(low, 64, 1), high),
        ):
            weight = DF[0, comp]
            near = jnp.where(lane < NZ, pltpu.roll(lo, BLOCK - NZ, 1), 0.0)
            far = jnp.where(lane < 2 * NZ, lo, 0.0)
            out[comp, :, 0:128] += weight * (near_weight * near - far_weight * far)
            near = jnp.where(lane >= BLOCK - NZ, pltpu.roll(hi, NZ, 1), 0.0)
            far = jnp.where(lane >= 2 * NZ, hi, 0.0)
            out[comp, :, 896:1024] += weight * (near_weight * near - far_weight * far)
        return 0

    looped(0, HALF, edges, 3)

    sub_row = lax.broadcasted_iota(jnp.int32, (8, 1024), 0)

    def outer(c, _):
        weight = DF[0, c]
        x = H[c]
        near = jnp.where(
            sub_row == 0, pltpu.roll(x, 1, 0), jnp.where(sub_row == 7, pltpu.roll(x, 7, 0), 0.0)
        )
        far = jnp.where(
            sub_row < 2, pltpu.roll(x, 2, 0), jnp.where(sub_row >= 6, pltpu.roll(x, 6, 0), 0.0)
        )
        out[c] += weight * (near_weight * near - far_weight * far)
        return 0

    for (c0, cn), pair in zip(CHUNKS, x_copies):
        for copy in pair:
            copy.wait_recv()
        looped(c0, cn, outer, 3)

    for pair in x_copies:
        for copy in pair:
            copy.wait_send()
    for copy in y_copies:
        copy.wait_send()


def per_device(
    state, diffusivity, log_prefactor, activation, heat, reactants, products, substeps, flame
):
    n, m = lax.axis_size("gx"), lax.axis_size("gy")
    anywhere = pl.BlockSpec(memory_space=pl.ANY)
    vmem, smem, dma = pltpu.VMEM, pltpu.SMEM, pltpu.SemaphoreType.DMA
    cells = state.shape[2]
    return pl.pallas_call(
        functools.partial(kernel, n, m),
        out_shape=pltpu.VMEM(state.shape, F32),
        in_specs=[anywhere] * 9,
        out_specs=pl.BlockSpec(memory_space=pltpu.VMEM),
        scratch_shapes=[
            vmem((COMP, 8, cells), F32),
            vmem((COMP, 8, cells), F32),
            vmem((2, HALF, 8, BLOCK), F32),
            vmem((2, HALF, 8, BLOCK), F32),
            smem((1, COMP), F32),
            vmem((RX,), F32),
            vmem((RX,), F32),
            vmem((RX,), F32),
            vmem((SP, 2 * RX), F32),
            vmem((SP, RX), F32),
            vmem((8, 8), jnp.int32),
            vmem((8, 8), jnp.int32),
            vmem((RROWS, WIDE), F32),
            vmem((RROWS, WIDE), F32),
            vmem((RROWS, 4 * CROWS), BF16),
            vmem((RROWS, 4 * CROWS), BF16),
            vmem((CROWS, 4 * RPAD), BF16),
            vmem((CROWS, 2 * RPAD), BF16),
            vmem((CROWS, SLOTS * BLOCK), F32),
            vmem((COMP, SLOTS, BLOCK), F32),
            vmem((8, SLOTS * BLOCK), jnp.int32),
            vmem((8, SLOTS * BLOCK), F32),
            vmem((6 * RPAD, WIDE), BF16),
            vmem((8, 8, BLOCK), jnp.int32),
            vmem((8, 8, BLOCK), jnp.int32),
            dma((2, len(CHUNKS))), dma((2, len(CHUNKS))), dma((2,)), dma((2,)), dma((9,)),
            *[pltpu.SemaphoreType.REGULAR] * 4,
        ],
        compiler_params=pltpu.CompilerParams(
            collective_id=0, has_side_effects=True, vmem_limit_bytes=VMEM_LIMIT
        ),
    )(
        state, diffusivity.reshape(1, -1), log_prefactor, activation,
        heat, reactants.T, products, substeps, flame,
    )


VMEM_LIMIT = 60 << 20


def solution(mesh):
    in_specs = (P(None, "gx", "gy"), P(), P(), P(), P(), P(), P(), P("gx", "gy"), P("gx", "gy"))
    return jax.shard_map(
        per_device, mesh=mesh, in_specs=in_specs, out_specs=P(None, "gx", "gy"), check_vma=False
    )
```
